256 devices in a mesh: region: 32 (over x, z), band: 8 (over y, core).
Axes of the slice: x: 4, y: 4, z: 8, core: 2. Of those that a mesh axis runs over, the one named last changes fastest.
Arguments:
- probes: bfloat16 [4, 4, 1024, 32768], P(None, None, 'band', 'region'), may hold values from -5 to 5
- filter_taps: float32 [2, 2, 17], replicated, may hold values from 0.02 to 1
- mixing: float32 [2, 4, 4], replicated, as said below
- nugget: float32 [4], replicated, may hold values from 0.3 to 1.5
- land_span: int32 [2, 1024, 32], P(None, 'band', 'region'), may hold values from 0 to 1024, as said below
Outputs:
- covariance_probes: bfloat16 [4, 4, 1024, 32768], P(None, None, 'band', 'region')
- quadratic: float32 [4, 3], replicated
The draws below stay inside these ranges and needn't reach their ends.
Inputs may be any that keep to these rules, and one draw needn't show every extreme that they name: Row r of region block b has land in the columns land_span[0, r, b] to land_span[1, r, b] - 1 of the block; land_span[0] <= land_span[1] everywhere. `mixing`: each of the 2 matrices is symmetric positive definite.
All inputs are finite; a program needn't handle non-finite values.
Results may differ from the reference program's by a relative error of at most 0.0062.
Values may be sent and summed in bfloat16 or wider, within the bound.
A program may use at most 128 MiB of HBM per device.

```python
import math
import jax
import jax.numpy as jnp
from jax import lax

PROBES = 4
VARS = 4
KERNELS = 2
HALF = 16
COLS_DEV = 1024
NY = 1024
NX = 32768
N_REGION = 32


def draw_mixing(key, part):
    factor = jax.random.normal(jax.random.fold_in(key, 11), (KERNELS, VARS, VARS), jnp.float32) * 0.5
    return jnp.einsum('kvr,kwr->kvw', factor, factor) + 0.3 * jnp.eye(VARS, dtype=jnp.float32)[None]


def draw_land_span(key, part):
    region = jnp.arange(N_REGION, dtype=jnp.int32)
    base = jax.random.randint(jax.random.fold_in(key, 21), (N_REGION,), COLS_DEV // 4, COLS_DEV + 1)
    base = base * (N_REGION + 2 * region) // (3 * N_REGION - 2)
    jitter = jax.random.randint(jax.random.fold_in(key, 24), (NY, N_REGION), -16, 17)
    extent = jnp.clip(base[None, :] + jitter, 0, COLS_DEV)
    anchor = jax.random.randint(jax.random.fold_in(key, 27), (NY, N_REGION), 0, 2)
    lower = jnp.where(anchor == 1, COLS_DEV - extent, 0)
    upper = jnp.where(anchor == 1, COLS_DEV, extent)
    row = jnp.arange(NY, dtype=jnp.int32)[:, None]
    east_row = jax.random.randint(jax.random.fold_in(key, 25), (N_REGION,), 0, NY)
    west_row = jax.random.randint(jax.random.fold_in(key, 26), (N_REGION,), 0, NY)
    lower = jnp.where(row == east_row[None, :], COLS_DEV, lower)
    upper = jnp.where(row == east_row[None, :], COLS_DEV, upper)
    lower = jnp.where(row == west_row[None, :], 0, lower)
    upper = jnp.where(row == west_row[None, :], 0, upper)
    return jnp.stack([lower, upper]).astype(jnp.int32)


def block_levels(own_key, shape, pieces, least, high):
    def one(dim, shards_of):
        draws = jax.random.uniform(jax.random.fold_in(jax.random.fold_in(own_key, 6), dim), (shards_of,), jnp.float32, least / len(pieces), high / len(pieces))
        return jnp.repeat(jnp.exp(draws), shape[dim] // shards_of).reshape((-1,) + (1,) * (len(shape) - dim - 1))

    gain = one(*pieces[0])
    for cut in pieces[1:]:
        gain = gain * one(*cut)
    return gain


def bell_draw(rng, shape, scale, limit, split=(), held_as=jnp.bfloat16):
    values = jax.random.normal(rng, shape, jnp.float32) * scale
    if len(split) > 0:
        values = block_levels(rng, shape, split, -0.22, 0.18) * values
    return jnp.clip(values, min=-limit, max=limit).astype(held_as)


def setup_inputs(seed: int = 0) -> dict:
    key_of = jax.random.split(jax.random.key(seed), 6)
    probes = bell_draw(key_of[0], (PROBES, VARS, NY, NX), 1.0, 5.0, ((2, 8), (3, 32)))
    filter_taps = jnp.clip(jnp.exp(jax.random.uniform(key_of[1], (KERNELS, 2, HALF + 1), jnp.float32, math.log(0.02), math.log(1.0))), 0.02, 1.0)
    mixing = draw_mixing(jax.random.fold_in(key_of[5], 71), 0)
    nugget = jnp.clip(jnp.exp(jax.random.uniform(key_of[3], (VARS,), jnp.float32, math.log(0.3), math.log(1.5))), 0.3, 1.5)
    land_span = draw_land_span(jax.random.fold_in(key_of[5], 71), 0)
    return dict(probes=probes, filter_taps=filter_taps, mixing=mixing, nugget=nugget, land_span=land_span)


def convolve_columns(plane, weights):
    half_width = (weights.shape[0] - 1) // 2
    count = plane.shape[1]
    padded = jnp.concatenate([plane[:, count - half_width:], plane, plane[:, :half_width]], axis=1)
    total = jnp.zeros_like(plane)
    for shift in range(weights.shape[0]):
        total = total + weights[shift] * padded[:, shift:shift + count]
    return total


def convolve_rows(plane, weights):
    half_width = (weights.shape[0] - 1) // 2
    count = plane.shape[0]
    padded = jnp.pad(plane, ((half_width, half_width), (0, 0)))
    total = jnp.zeros_like(plane)
    for shift in range(weights.shape[0]):
        total = total + weights[shift] * padded[shift:shift + count, :]
    return total


def reference(probes, filter_taps, mixing, nugget, land_span):
    rounded = lax.optimization_barrier(filter_taps.astype(jnp.bfloat16)).astype(jnp.float32)
    mirrored = jnp.concatenate([rounded[:, :, :0:-1], rounded], axis=2)
    column = jnp.arange(NX, dtype=jnp.int32)
    region_of = (column // COLS_DEV).astype(jnp.int32)
    local_col = (column % COLS_DEV).astype(jnp.int32)
    lower = land_span[0][:, region_of]
    upper = land_span[1][:, region_of]
    landed = (local_col[None, :] >= lower) & (local_col[None, :] < upper)

    def one_probe(field):
        masked = jnp.where(landed[None], field, jnp.zeros((), field.dtype)).astype(jnp.float32)
        total = nugget[:, None, None] * masked
        quad_terms = []
        for kernel in range(KERNELS):
            mixed = jnp.zeros_like(masked)
            for source in range(VARS):
                across = convolve_columns(masked[source], mirrored[kernel, 0])
                across = lax.optimization_barrier(across.astype(jnp.bfloat16)).astype(jnp.float32)
                smooth = convolve_rows(across, mirrored[kernel, 1])
                mixed = mixed + mixing[kernel, :, source][:, None, None] * smooth[None]
            quad_terms.append(jnp.sum(mixed * masked))
            total = total + mixed
        quad_terms.append(jnp.sum(nugget[:, None, None] * masked * masked))
        output = jnp.where(landed[None], total, jnp.zeros((), total.dtype)).astype(jnp.bfloat16)
        return output, jnp.stack(quad_terms) / (NY * COLS_DEV)

    outputs, quadratic = lax.map(one_probe, probes)
    return outputs, quadratic
```

```python
import functools

import jax
import jax.numpy as jnp
from jax import lax
from jax.experimental import pallas as pl
from jax.experimental.pallas import tpu as pltpu
from jax.sharding import PartitionSpec as P

MESH = pl.DeviceIdType.MESH
BF16 = jnp.bfloat16
F32 = jnp.float32

PROBES, VARS, KERNELS, HALF = 4, 4, 2, 16
PLANES = PROBES * VARS
LANES = 128
TILE = 32
WINDOW = TILE + 2 * HALF
GROUP = LANES // HALF


def toeplitz(distance, tap):
    reach = jnp.abs(distance - HALF)
    total = jnp.zeros(distance.shape, F32)
    for step in range(HALF + 1):
        total = jnp.where(reach == step, tap(step), total)
    return total


def lane_of(rows):
    return lax.broadcasted_iota(jnp.int32, (rows, LANES), 1)


def kernel(
    probes, taps, mixing, nugget, span, out, quad,
    held, land, padded, across, staged, column_filter, row_filter, edges,
    row_halo, col_halo, corner_halo, partial, shares, slots_a, slots_b, slots_c,
    load_sem, row_send, row_recv, col_send, col_recv, corner_send, corner_recv,
    store_sem, share_send, share_recv,
):
    rows, cols = held.shape[1:]
    blocks = cols // LANES
    regions, bands = lax.axis_size("region"), lax.axis_size("band")
    across_z = 8 if regions % 8 == 0 else regions
    across_x = regions // across_z
    region, band = lax.axis_index("region"), lax.axis_index("band")
    east, west = lax.rem(region + 1, regions), lax.rem(region + regions - 1, regions)
    south, north = lax.rem(band + 1, bands), lax.rem(band + bands - 1, bands)
    base_z = lax.div(region, across_z) * across_z
    at_z = lax.rem(region, across_z)

    band_peers = [(region, lax.rem(band + d, bands)) for d in range(1, bands)]
    z_peers = [(base_z + lax.rem(at_z + d, across_z), band) for d in range(1, across_z)]
    x_peers = [(lax.rem(region + d * across_z, regions), band) for d in range(1, across_x)]
    corners = [(east, south), (east, north), (west, south), (west, north)]
    greeted = band_peers + z_peers + x_peers + [(east, band), (west, band)] + corners

    loads = [
        pltpu.make_async_copy(
            probes.at[pl.ds(VARS * p, VARS)], held.at[pl.ds(VARS * p, VARS)], load_sem.at[p]
        )
        for p in range(PROBES)
    ]
    for load in loads:
        load.start()
    barrier = pltpu.get_barrier_semaphore()
    for peer in greeted:
        pl.semaphore_signal(barrier, inc=1, device_id=peer, device_id_type=MESH)

    def by_row(entry):
        line = span[entry].astype(F32)
        return jnp.transpose(jnp.broadcast_to(line, (LANES, rows)))

    lower, upper = by_row(0), by_row(1)
    for block in range(blocks):
        column = (lane_of(rows) + block * LANES).astype(F32)
        inside = (column >= lower) & (column < upper)
        land[:, block * LANES : (block + 1) * LANES] = jnp.where(inside, 1.0, 0.0).astype(BF16)

    def rounded(k, axis):
        return lambda step: jnp.full((1, 1), taps[k, axis, step], F32).astype(BF16).astype(F32)

    shape = (2 * LANES, LANES)
    offset = lax.broadcasted_iota(jnp.int32, shape, 0) - lax.broadcasted_iota(jnp.int32, shape, 1)
    for k in range(KERNELS):
        column_filter[:, k * LANES : (k + 1) * LANES] = toeplitz(offset, rounded(k, 0)).astype(BF16)
    shape = (TILE, LANES)
    lane = lax.broadcasted_iota(jnp.int32, shape, 1)
    offset = lax.rem(lane, WINDOW) - lax.broadcasted_iota(jnp.int32, shape, 0)
    for k in range(KERNELS):
        pattern = toeplitz(offset, rounded(k, 1))
        for v in range(VARS):
            for w in range(0, VARS, 2):
                gains = jnp.where(lane < WINDOW, mixing[k, v, w], mixing[k, v, w + 1])
                row_filter[k, v * TILE : (v + 1) * TILE, w * WINDOW : (w + 2) * WINDOW] = (
                    gains * pattern
                ).astype(BF16)

    lanes = lane_of(rows)
    zero = jnp.zeros((rows, LANES), BF16)

    def shifted(block, first, store):
        previous = first
        for j in range(blocks):
            current = pltpu.roll(block(j), HALF, 1)
            store(j, jnp.where(lane_of(current.shape[0]) < HALF, previous, current))
            previous = current
        return previous

    def mask_planes(p):
        loads[p].wait()
        for v in range(VARS):
            q = VARS * p + v
            held[q] = held[q] * land[...]

    def row_copies(p):
        some = pl.ds(VARS * p, VARS)
        return [
            pltpu.make_async_remote_copy(
                held.at[some, pl.ds(rows - HALF, HALF)], row_halo.at[0, some],
                row_send.at[0, p], row_recv.at[0, p], device_id=(region, south),
                device_id_type=MESH,
            ),
            pltpu.make_async_remote_copy(
                held.at[some, pl.ds(0, HALF)], row_halo.at[1, some],
                row_send.at[1, p], row_recv.at[1, p], device_id=(region, north),
                device_id_type=MESH,
            ),
        ]

    def edge_copies(g):
        copies = []
        for side, target in ((0, west), (1, east)):
            copies.append(
                pltpu.make_async_remote_copy(
                    edges.at[side, g], col_halo.at[1 - side, g],
                    col_send.at[side, g], col_recv.at[1 - side, g],
                    device_id=(target, band), device_id_type=MESH,
                )
            )
        for side, target in ((0, west), (1, east)):
            for end, line in ((0, north), (1, south)):
                copies.append(
                    pltpu.make_async_remote_copy(
                        edges.at[side, g, pl.ds(end * (rows - HALF), HALF)],
                        corner_halo.at[1 - side, 1 - end, g],
                        corner_send.at[side, end, g], corner_recv.at[1 - side, 1 - end, g],
                        device_id=(target, line), device_id_type=MESH,
                    )
                )
        return copies

    def pack_edges(g):
        west_edge, east_edge = zero, zero
        for a in range(GROUP):
            q = GROUP * g + a
            both = jnp.where(lanes < HALF, held[q, :, :LANES], held[q, :, cols - LANES :])
            both = pltpu.roll(both, a * HALF, 1) if a else both
            slot = lax.div(lanes, HALF)
            west_edge = jnp.where(slot == a, both, west_edge)
            east_edge = jnp.where(slot == (a - 1) % GROUP, both, east_edge)
        edges[0, g] = west_edge
        edges[1, g] = east_edge

    row_moves, edge_moves = [], []
    for p in range(PROBES):
        mask_planes(p)
        if p == 0:
            pl.semaphore_wait(barrier, len(greeted))
        row_moves.append(row_copies(p))
        for move in row_moves[-1]:
            move.start()
        if (p + 1) * VARS % GROUP == 0:
            g = p * VARS // GROUP
            pack_edges(g)
            edge_moves.append(edge_copies(g))
            for move in edge_moves[-1]:
                move.start()

    def shift_planes(number, carry):
        for u in range(4):
            q = 4 * number + u

            def store(j, value):
                padded[q, HALF : HALF + rows, j * LANES : (j + 1) * LANES] = value

            last = shifted(lambda j: held[q, :, j * LANES : (j + 1) * LANES], zero, store)
            store(blocks, jnp.where(lanes < HALF, last, zero))
        return carry

    lax.fori_loop(0, PLANES // 4, shift_planes, 0)

    def filter_columns(number, carry, chosen):
        for u in range(4):
            q = 4 * number + u
            for j in chosen:
                window = padded[q, HALF : HALF + rows, j * LANES : (j + 2) * LANES]
                both = jnp.dot(
                    window, column_filter[...], preferred_element_type=F32
                ).astype(BF16)
                for k in range(KERNELS):
                    across[k, q, HALF : HALF + rows, j * LANES : (j + 1) * LANES] = both[
                        :, k * LANES : (k + 1) * LANES
                    ]
        return carry

    lax.fori_loop(
        0, PLANES // 4, functools.partial(filter_columns, chosen=range(1, blocks - 1)), 0
    )

    def unpack(west_halo, east_halo, a):
        slot = lax.div(lane_of(west_halo.shape[0]), HALF)
        both = jnp.where(slot == a, east_halo, west_halo)
        turn = (LANES - (a - 1) * HALF) % LANES
        return pltpu.roll(both, turn, 1) if turn else both

    for g in range(PLANES // GROUP):
        for move in edge_moves[g][:2]:
            move.wait_recv()
        for a in range(GROUP):
            q = GROUP * g + a
            halo = unpack(col_halo[0, g], col_halo[1, g], a)
            own = pl.ds(HALF, rows)
            padded[q, own, :LANES] = jnp.where(lanes < HALF, halo, padded[q, own, :LANES])
            tail = jnp.where(lanes < 2 * HALF, halo, zero)
            padded[q, own, cols:] = jnp.where(lanes < HALF, padded[q, own, cols:], tail)
    lax.fori_loop(0, PLANES // 4, functools.partial(filter_columns, chosen=(0, blocks - 1)), 0)

    width = 2 * LANES
    partial[...] = jnp.zeros_like(partial)

    def folded(value):
        value = jnp.sum(value.reshape(-1, 8, width), axis=0)
        return value[:, :LANES] + value[:, LANES:]

    def finish_tiles(p, tiles):
        first = VARS * p
        for tile in tiles:
            own = pl.ds(tile * TILE, TILE)
            for chunk in range(cols // width):
                part = pl.ds(chunk * width, width)
                terms = []
                for k in range(KERNELS):
                    stack = jnp.concatenate(
                        [
                            across[k, first + w, pl.ds(tile * TILE, WINDOW), part]
                            for w in range(VARS)
                        ],
                        axis=0,
                    )
                    terms.append(jnp.dot(row_filter[k], stack, preferred_element_type=F32))
                keep = land[own, part] != 0
                sums = [jnp.zeros((8, LANES), F32) for _ in range(KERNELS + 1)]
                for v in range(VARS):
                    local = held[first + v, own, part].astype(F32)
                    noise = nugget[v] * local
                    mixed = [term[v * TILE : (v + 1) * TILE] for term in terms]
                    total = (mixed[0] + mixed[1] + noise).astype(BF16)
                    staged[first + v, own, part] = jnp.where(keep, total, jnp.zeros_like(total))
                    for k, term in enumerate(mixed + [noise]):
                        sums[k] = sums[k] + folded(term * local)
                for k in range(KERNELS + 1):
                    partial[k, p] = partial[k, p] + sums[k]

    def inner_tiles(p, carry):
        finish_tiles(p, range(1, rows // TILE - 1))
        return carry

    lax.fori_loop(0, PROBES, inner_tiles, 0)

    for g in range(PLANES // GROUP):
        for move in edge_moves[g][2:]:
            move.wait_recv()
    for p in range(PROBES):
        for move in row_moves[p]:
            move.wait_recv()

    beyond = [(band > 0).astype(F32).astype(BF16), (band < bands - 1).astype(F32).astype(BF16)]
    short = lane_of(HALF)
    none = jnp.zeros((HALF, LANES), BF16)
    def halo_rows(g, carry):
        for a in range(GROUP):
            q = GROUP * g + a
            for end, place in ((0, 0), (1, HALF + rows)):
                halo = unpack(corner_halo[0, end, g], corner_halo[1, end, g], a)

                def store(j, value):
                    padded[q, place : place + HALF, j * LANES : (j + 1) * LANES] = (
                        value * beyond[end]
                    )

                last = shifted(
                    lambda j: row_halo[end, q, :, j * LANES : (j + 1) * LANES], halo, store
                )
                tail = jnp.where(short < 2 * HALF, halo, none)
                store(blocks, jnp.where(short < HALF, last, tail))
        return carry

    lax.fori_loop(0, PLANES // GROUP, halo_rows, 0)

    def filter_halo(number, carry):
        ends = (0, HALF + rows)
        for j in range(blocks):
            part = slice(j * LANES, (j + 2) * LANES)
            window = jnp.concatenate(
                [padded[4 * number + u, at : at + HALF, part] for u in range(4) for at in ends],
                axis=0,
            )
            both = jnp.dot(window, column_filter[...], preferred_element_type=F32).astype(BF16)
            for u in range(4):
                for end, at in enumerate(ends):
                    start = (2 * u + end) * HALF
                    for k in range(KERNELS):
                        across[
                            k, 4 * number + u, at : at + HALF, j * LANES : (j + 1) * LANES
                        ] = both[start : start + HALF, k * LANES : (k + 1) * LANES]
        return carry

    lax.fori_loop(0, PLANES // 4, filter_halo, 0)

    def outer_tiles(p, carry):
        finish_tiles(p, (0, rows // TILE - 1))
        some = pl.ds(VARS * p, VARS)
        pltpu.make_async_copy(staged.at[some], out.at[some], store_sem.at[p]).start()
        return carry

    lax.fori_loop(0, PROBES, outer_tiles, 0)

    value = jnp.sum(partial[...].reshape(-1, 8, LANES), axis=1)
    for number, (peers, slots) in enumerate(
        ((band_peers, slots_a), (z_peers, slots_b), (x_peers, slots_c))
    ):
        if not peers:
            continue
        shares[number] = value
        moves = [
            pltpu.make_async_remote_copy(
                shares.at[number], slots.at[d], share_send.at[number, d], share_recv.at[number, d],
                device_id=peer, device_id_type=MESH,
            )
            for d, peer in enumerate(peers)
        ]
        for move in moves:
            move.start()
        for d, move in enumerate(moves):
            move.wait()
        for d in range(len(peers)):
            value = value + slots[d]
    value = jnp.sum(value, axis=1, keepdims=True) * (1.0 / (bands * rows * cols))
    for k in range(KERNELS + 1):
        quad[:, k : k + 1] = value[k * PROBES : (k + 1) * PROBES]

    for moves in row_moves + edge_moves:
        for move in moves:
            move.wait_send()
    for p in range(PROBES):
        some = pl.ds(VARS * p, VARS)
        pltpu.make_async_copy(staged.at[some], out.at[some], store_sem.at[p]).wait()


def per_device(probes, filter_taps, mixing, nugget, land_span):
    rows, cols = probes.shape[2:]
    bands = lax.axis_size("band")
    any_space = pl.BlockSpec(memory_space=pl.ANY)
    scalars = pl.BlockSpec(memory_space=pltpu.SMEM)
    vector = pl.BlockSpec(memory_space=pltpu.VMEM)
    count = (KERNELS + 1) * PROBES
    dma = pltpu.SemaphoreType.DMA
    out, quadratic = pl.pallas_call(
        kernel,
        out_shape=(
            jax.ShapeDtypeStruct((PLANES, rows, cols), BF16),
            jax.ShapeDtypeStruct((PROBES, KERNELS + 1), F32),
        ),
        in_specs=[any_space, scalars, scalars, scalars, vector],
        out_specs=(any_space, vector),
        scratch_shapes=[
            pltpu.VMEM((PLANES, rows, cols), BF16),
            pltpu.VMEM((rows, cols), BF16),
            pltpu.VMEM((PLANES, rows + 2 * HALF, cols + LANES), BF16),
            pltpu.VMEM((KERNELS, PLANES, rows + 2 * HALF, cols), BF16),
            pltpu.VMEM((PLANES, rows, cols), BF16),
            pltpu.VMEM((2 * LANES, KERNELS * LANES), BF16),
            pltpu.VMEM((KERNELS, VARS * TILE, VARS * WINDOW), BF16),
            pltpu.VMEM((2, PLANES // GROUP, rows, LANES), BF16),
            pltpu.VMEM((2, PLANES, HALF, cols), BF16),
            pltpu.VMEM((2, PLANES // GROUP, rows, LANES), BF16),
            pltpu.VMEM((2, 2, PLANES // GROUP, HALF, LANES), BF16),
            pltpu.VMEM((KERNELS + 1, PROBES, 8, LANES), F32),
            pltpu.VMEM((3, count, LANES), F32),
            pltpu.VMEM((max(bands - 1, 1), count, LANES), F32),
            pltpu.VMEM((7, count, LANES), F32),
            pltpu.VMEM((3, count, LANES), F32),
            dma((PROBES,)),
            dma((2, PROBES)),
            dma((2, PROBES)),
            dma((2, PLANES // GROUP)),
            dma((2, PLANES // GROUP)),
            dma((2, 2, PLANES // GROUP)),
            dma((2, 2, PLANES // GROUP)),
            dma((PROBES,)),
            dma((3, 7)),
            dma((3, 7)),
        ],
        compiler_params=pltpu.CompilerParams(
            collective_id=0, has_side_effects=True, vmem_limit_bytes=56 * 1024 * 1024
        ),
    )(
        probes.reshape(PLANES, rows, cols),
        filter_taps,
        mixing,
        nugget,
        jnp.transpose(land_span, (0, 2, 1)),
    )
    return out.reshape(PROBES, VARS, rows, cols), quadratic


def solution(mesh):
    return jax.shard_map(
        per_device,
        mesh=mesh,
        in_specs=(P(None, None, "band", "region"), P(), P(), P(), P(None, "band", "region")),
        out_specs=(P(None, None, "band", "region"), P()),
        check_vma=False,
    )
```

```python
import functools

import jax
import jax.numpy as jnp
from jax import lax
from jax.experimental import pallas as pl
from jax.experimental.pallas import tpu as pltpu
from jax.sharding import PartitionSpec as P

MESH = pl.DeviceIdType.MESH
BF16 = jnp.bfloat16
F32 = jnp.float32

PROBES, VARS, KERNELS, HALF = 4, 4, 2, 16
PLANES = PROBES * VARS
LANES = 128
TILE = 32
WINDOW = TILE + 2 * HALF
GROUP = LANES // HALF


def toeplitz(distance, tap):
    reach = jnp.abs(distance - HALF)
    total = jnp.zeros(distance.shape, F32)
    for step in range(HALF + 1):
        total = jnp.where(reach == step, tap(step), total)
    return total


def lane_of(rows):
    return lax.broadcasted_iota(jnp.int32, (rows, LANES), 1)


def kernel(
    probes, taps, mixing, nugget, span, out, quad,
    held, land, padded, across, column_filter, row_filter, edges,
    row_halo, col_halo, corner_halo, partial, shares, slots_a, slots_b,
    load_sem, row_send, row_recv, col_send, col_recv, corner_send, corner_recv,
    share_send, share_recv,
):
    rows, cols = held.shape[1:]
    blocks = cols // LANES
    regions, bands = lax.axis_size("region"), lax.axis_size("band")
    across_z = 8 if regions % 8 == 0 else regions
    across_x = regions // across_z
    region, band = lax.axis_index("region"), lax.axis_index("band")
    east, west = lax.rem(region + 1, regions), lax.rem(region + regions - 1, regions)
    south, north = lax.rem(band + 1, bands), lax.rem(band + bands - 1, bands)
    base_z = lax.div(region, across_z) * across_z
    at_z = lax.rem(region, across_z)

    cores = 2
    strips = bands // cores
    at_y, core = lax.div(band, cores), lax.rem(band, cores)
    near = [
        (base_z + lax.rem(at_z + d // cores, across_z), at_y * cores + lax.rem(core + d, cores))
        for d in range(1, across_z * cores)
    ]
    far = [
        (lax.rem(region + d // strips * across_z, regions), lax.rem(band + d % strips * cores, bands))
        for d in range(1, across_x * strips)
    ]
    corners = [(east, south), (east, north), (west, south), (west, north)]
    greeted = near + far + [(region, south), (region, north), (east, band), (west, band)] + corners

    loads = [
        pltpu.make_async_copy(
            probes.at[pl.ds(VARS * p, VARS)], held.at[pl.ds(VARS * p, VARS)], load_sem.at[p]
        )
        for p in range(PROBES)
    ]
    for load in loads:
        load.start()
    barrier = pltpu.get_barrier_semaphore()
    for peer in greeted:
        pl.semaphore_signal(barrier, inc=1, device_id=peer, device_id_type=MESH)

    def by_row(entry):
        line = span[entry].astype(F32)
        return jnp.transpose(jnp.broadcast_to(line, (LANES, rows)))

    lower, upper = by_row(0), by_row(1)
    for block in range(blocks):
        column = (lane_of(rows) + block * LANES).astype(F32)
        inside = (column >= lower) & (column < upper)
        land[:, block * LANES : (block + 1) * LANES] = jnp.where(inside, 1.0, 0.0).astype(BF16)

    def rounded(k, axis):
        return lambda step: jnp.full((1, 1), taps[k, axis, step], F32).astype(BF16).astype(F32)

    shape = (2 * LANES, LANES)
    offset = lax.broadcasted_iota(jnp.int32, shape, 0) - lax.broadcasted_iota(jnp.int32, shape, 1)
    for k in range(KERNELS):
        column_filter[:, k * LANES : (k + 1) * LANES] = toeplitz(offset, rounded(k, 0)).astype(BF16)
    shape = (TILE, LANES)
    lane = lax.broadcasted_iota(jnp.int32, shape, 1)
    offset = lax.rem(lane, WINDOW) - lax.broadcasted_iota(jnp.int32, shape, 0)
    for k in range(KERNELS):
        pattern = toeplitz(offset, rounded(k, 1))
        for v in range(VARS):
            for w in range(0, VARS, 2):
                gains = jnp.where(lane < WINDOW, mixing[k, v, w], mixing[k, v, w + 1])
                row_filter[k, v * TILE : (v + 1) * TILE, w * WINDOW : (w + 2) * WINDOW] = (
                    gains * pattern
                ).astype(BF16)

    lanes = lane_of(rows)
    zero = jnp.zeros((rows, LANES), BF16)
    own = slice(HALF, HALF + rows)

    def columns(j, count=1):
        return slice(j * LANES, (j + count) * LANES)

    def shifted(block, first, store):
        previous = first
        for j in range(blocks):
            current = pltpu.roll(block(j), HALF, 1)
            store(j, jnp.where(lane_of(current.shape[0]) < HALF, previous, current))
            previous = current
        return previous

    def row_copies(p):
        some = pl.ds(VARS * p, VARS)
        return [
            pltpu.make_async_remote_copy(
                held.at[some, pl.ds(rows - HALF, HALF)], row_halo.at[0, some],
                row_send.at[0, p], row_recv.at[0, p], device_id=(region, south),
                device_id_type=MESH,
            ),
            pltpu.make_async_remote_copy(
                held.at[some, pl.ds(0, HALF)], row_halo.at[1, some],
                row_send.at[1, p], row_recv.at[1, p], device_id=(region, north),
                device_id_type=MESH,
            ),
        ]

    def edge_copies(g):
        copies = []
        for side, target in ((0, west), (1, east)):
            copies.append(
                pltpu.make_async_remote_copy(
                    edges.at[side, g], col_halo.at[1 - side, g],
                    col_send.at[side, g], col_recv.at[1 - side, g],
                    device_id=(target, band), device_id_type=MESH,
                )
            )
        for side, target in ((0, west), (1, east)):
            for end, line in ((0, north), (1, south)):
                copies.append(
                    pltpu.make_async_remote_copy(
                        edges.at[side, g, pl.ds(end * (rows - HALF), HALF)],
                        corner_halo.at[1 - side, 1 - end, g],
                        corner_send.at[side, end, g], corner_recv.at[1 - side, 1 - end, g],
                        device_id=(target, line), device_id_type=MESH,
                    )
                )
        return copies

    def mask_borders(q, a, packed):
        for place in (slice(0, HALF), slice(rows - HALF, rows)):
            held[q, place] = held[q, place] * land[place]
        both = jnp.where(lanes < HALF, held[q, :, columns(0)], held[q, :, columns(blocks - 1)])
        both = both * jnp.where(lanes < HALF, land[:, columns(0)], land[:, columns(blocks - 1)])
        both = pltpu.roll(both, a * HALF, 1) if a else both
        slot = lax.div(lanes, HALF)
        return [
            jnp.where(slot == a, both, packed[0]),
            jnp.where(slot == (a - 1) % GROUP, both, packed[1]),
        ]

    def mask_and_shift(q):
        inner = slice(HALF, rows - HALF)

        def block(j):
            value = held[q, :, columns(j)] * land[:, columns(j)]
            held[q, inner, columns(j)] = value[inner]
            return value

        def store(j, value):
            padded[q, own, columns(j)] = value

        last = shifted(block, zero, store)
        store(blocks, jnp.where(lanes < HALF, last, zero))

    def filter_plane(q, chosen):
        for j in chosen:
            both = jnp.dot(
                padded[q, own, columns(j, 2)], column_filter[...], preferred_element_type=F32
            ).astype(BF16)
            for k in range(KERNELS):
                across[k, q, own, columns(j)] = both[:, columns(k)]

    row_moves, edge_moves = [], []
    packed = [zero, zero]
    for p in range(PROBES):
        loads[p].wait()
        for q in range(VARS * p, VARS * (p + 1)):
            packed = mask_borders(q, q % GROUP, packed)
        if p == 0:
            pl.semaphore_wait(barrier, len(greeted))
        row_moves.append(row_copies(p))
        for move in row_moves[-1]:
            move.start()
        if (p + 1) * VARS % GROUP == 0:
            g = p * VARS // GROUP
            edges[0, g], edges[1, g] = packed
            packed = [zero, zero]
            edge_moves.append(edge_copies(g))
            for move in edge_moves[-1]:
                move.start()
    for q in range(PLANES):
        mask_and_shift(q)
        filter_plane(q, range(1, blocks - 1))

    width = 2 * LANES
    partial[...] = jnp.zeros_like(partial)

    def folded(value):
        value = jnp.sum(value.reshape(-1, 8, width), axis=0)
        return value[:, :LANES] + value[:, LANES:]

    def finish_tiles(p, tiles, chunks):
        first = VARS * p
        for tile in tiles:
            own = pl.ds(tile * TILE, TILE)
            for chunk in chunks:
                part = pl.ds(chunk * width, width)
                terms = []
                for k in range(KERNELS):
                    stack = jnp.concatenate(
                        [
                            across[k, first + w, pl.ds(tile * TILE, WINDOW), part]
                            for w in range(VARS)
                        ],
                        axis=0,
                    )
                    terms.append(jnp.dot(row_filter[k], stack, preferred_element_type=F32))
                keep = land[own, part] != 0
                sums = [jnp.zeros((8, LANES), F32) for _ in range(KERNELS + 1)]
                for v in range(VARS):
                    local = held[first + v, own, part].astype(F32)
                    noise = nugget[v] * local
                    mixed = [term[v * TILE : (v + 1) * TILE] for term in terms]
                    total = (mixed[0] + mixed[1] + noise).astype(BF16)
                    out[first + v, own, part] = jnp.where(keep, total, jnp.zeros_like(total))
                    for k, term in enumerate(mixed + [noise]):
                        sums[k] = sums[k] + folded(term * local)
                for k in range(KERNELS + 1):
                    partial[k, p] = partial[k, p] + sums[k]

    def inner_tiles(p, carry, chunks):
        finish_tiles(p, range(1, rows // TILE - 1), chunks)
        return carry

    chunks = cols // width
    middle, ends = range(1, chunks - 1), (0, chunks - 1)
    lax.fori_loop(0, PROBES, functools.partial(inner_tiles, chunks=middle), 0)

    def unpack(west_halo, east_halo, a):
        slot = lax.div(lane_of(west_halo.shape[0]), HALF)
        both = jnp.where(slot == a, east_halo, west_halo)
        turn = (1 - a) % GROUP * HALF
        return pltpu.roll(both, turn, 1) if turn else both

    for moves in edge_moves:
        for move in moves[:2]:
            move.wait_recv()

    def outer_columns(g, carry):
        for a in range(GROUP):
            q = GROUP * g + a
            halo = unpack(col_halo[0, g], col_halo[1, g], a)
            padded[q, own, columns(0)] = jnp.where(lanes < HALF, halo, padded[q, own, columns(0)])
            tail = jnp.where(lanes < 2 * HALF, halo, zero)
            padded[q, own, columns(blocks)] = jnp.where(
                lanes < HALF, padded[q, own, columns(blocks)], tail
            )
        for a in range(GROUP):
            filter_plane(GROUP * g + a, (0, blocks - 1))
        return carry

    lax.fori_loop(0, PLANES // GROUP, outer_columns, 0)

    lax.fori_loop(0, PROBES, functools.partial(inner_tiles, chunks=ends), 0)

    for g in range(PLANES // GROUP):
        for move in edge_moves[g][2:]:
            move.wait_recv()
    for p in range(PROBES):
        for move in row_moves[p]:
            move.wait_recv()

    beyond = [(band > 0).astype(F32).astype(BF16), (band < bands - 1).astype(F32).astype(BF16)]
    short = lane_of(HALF)
    none = jnp.zeros((HALF, LANES), BF16)
    def halo_rows(g, carry):
        for a in range(GROUP):
            q = GROUP * g + a
            for end, place in ((0, 0), (1, HALF + rows)):
                halo = unpack(corner_halo[0, end, g], corner_halo[1, end, g], a)

                def store(j, value):
                    padded[q, place : place + HALF, j * LANES : (j + 1) * LANES] = (
                        value * beyond[end]
                    )

                last = shifted(
                    lambda j: row_halo[end, q, :, j * LANES : (j + 1) * LANES], halo, store
                )
                tail = jnp.where(short < 2 * HALF, halo, none)
                store(blocks, jnp.where(short < HALF, last, tail))
        return carry

    lax.fori_loop(0, PLANES // GROUP, halo_rows, 0)

    def filter_halo(number, carry):
        ends = (0, HALF + rows)
        for j in range(blocks):
            part = slice(j * LANES, (j + 2) * LANES)
            window = jnp.concatenate(
                [padded[4 * number + u, at : at + HALF, part] for u in range(4) for at in ends],
                axis=0,
            )
            both = jnp.dot(window, column_filter[...], preferred_element_type=F32).astype(BF16)
            for u in range(4):
                for end, at in enumerate(ends):
                    start = (2 * u + end) * HALF
                    for k in range(KERNELS):
                        across[
                            k, 4 * number + u, at : at + HALF, j * LANES : (j + 1) * LANES
                        ] = both[start : start + HALF, k * LANES : (k + 1) * LANES]
        return carry

    lax.fori_loop(0, PLANES // 4, filter_halo, 0)

    def outer_tiles(p, carry):
        finish_tiles(p, (0, rows // TILE - 1), range(chunks))
        return carry

    lax.fori_loop(0, PROBES, outer_tiles, 0)

    count = (KERNELS + 1) * PROBES
    value = jnp.sum(partial[...].reshape(count, 8, LANES), axis=1)
    value = jnp.sum(value, axis=1, keepdims=True)
    row = lax.broadcasted_iota(jnp.int32, (count, LANES), 0)
    value = jnp.sum(jnp.where(lane_of(count) == row, value, 0.0), axis=0, keepdims=True)
    share_moves = []
    for number, (peers, slots) in enumerate(((near, slots_a), (far, slots_b))):
        if not peers:
            continue
        shares[number] = value
        moves = [
            pltpu.make_async_remote_copy(
                shares.at[number], slots.at[d], share_send.at[number, d], share_recv.at[number, d],
                device_id=peer, device_id_type=MESH,
            )
            for d, peer in enumerate(peers)
        ]
        for move in moves:
            move.start()
        for move in moves:
            move.wait_recv()
        value = value + jnp.sum(slots[: len(peers)], axis=0)
        share_moves.append(moves)
    value = jnp.broadcast_to(value * (1.0 / (bands * rows * cols)), (PROBES, LANES))
    lane = lane_of(PROBES)
    row = lax.broadcasted_iota(jnp.int32, (PROBES, LANES), 0)
    for k in range(KERNELS + 1):
        chosen = jnp.where(lane == k * PROBES + row, value, 0.0)
        quad[:, k : k + 1] = jnp.sum(chosen, axis=1, keepdims=True)

    for moves in row_moves + edge_moves + share_moves:
        for move in moves:
            move.wait_send()


def per_device(probes, filter_taps, mixing, nugget, land_span):
    rows, cols = probes.shape[2:]
    any_space = pl.BlockSpec(memory_space=pl.ANY)
    scalars = pl.BlockSpec(memory_space=pltpu.SMEM)
    vector = pl.BlockSpec(memory_space=pltpu.VMEM)
    dma = pltpu.SemaphoreType.DMA
    out, quadratic = pl.pallas_call(
        kernel,
        out_shape=(
            pltpu.VMEM((PLANES, rows, cols), BF16),
            pltpu.VMEM((PROBES, KERNELS + 1), F32),
        ),
        in_specs=[any_space, scalars, scalars, scalars, vector],
        out_specs=(vector, vector),
        scratch_shapes=[
            pltpu.VMEM((PLANES, rows, cols), BF16),
            pltpu.VMEM((rows, cols), BF16),
            pltpu.VMEM((PLANES, rows + 2 * HALF, cols + LANES), BF16),
            pltpu.VMEM((KERNELS, PLANES, rows + 2 * HALF, cols), BF16),
            pltpu.VMEM((2 * LANES, KERNELS * LANES), BF16),
            pltpu.VMEM((KERNELS, VARS * TILE, VARS * WINDOW), BF16),
            pltpu.VMEM((2, PLANES // GROUP, rows, LANES), BF16),
            pltpu.VMEM((2, PLANES, HALF, cols), BF16),
            pltpu.VMEM((2, PLANES // GROUP, rows, LANES), BF16),
            pltpu.VMEM((2, 2, PLANES // GROUP, HALF, LANES), BF16),
            pltpu.VMEM((KERNELS + 1, PROBES, 8, LANES), F32),
            pltpu.VMEM((2, 1, LANES), F32),
            pltpu.VMEM((15, 1, LANES), F32),
            pltpu.VMEM((15, 1, LANES), F32),
            dma((PROBES,)),
            dma((2, PROBES)),
            dma((2, PROBES)),
            dma((2, PLANES // GROUP)),
            dma((2, PLANES // GROUP)),
            dma((2, 2, PLANES // GROUP)),
            dma((2, 2, PLANES // GROUP)),
            dma((2, 15)),
            dma((2, 15)),
        ],
        compiler_params=pltpu.CompilerParams(
            collective_id=0, has_side_effects=True, vmem_limit_bytes=56 * 1024 * 1024
        ),
    )(
        probes.reshape(PLANES, rows, cols),
        filter_taps,
        mixing,
        nugget,
        jnp.transpose(land_span, (0, 2, 1)),
    )
    return out.reshape(PROBES, VARS, rows, cols), quadratic


def solution(mesh):
    return jax.shard_map(
        per_device,
        mesh=mesh,
        in_specs=(P(None, None, "band", "region"), P(), P(), P(), P(None, "band", "region")),
        out_specs=(P(None, None, "band", "region"), P()),
        check_vma=False,
    )
```

```python
import functools

import jax
import jax.numpy as jnp
from jax import lax
from jax.experimental import pallas as pl
from jax.experimental.pallas import tpu as pltpu
from jax.sharding import PartitionSpec as P

MESH = pl.DeviceIdType.MESH
BF16 = jnp.bfloat16
F32 = jnp.float32

PROBES, VARS, KERNELS, HALF = 4, 4, 2, 16
PLANES = PROBES * VARS
LANES = 128
TILE = 32
WINDOW = TILE + 2 * HALF
GROUP = LANES // HALF


def toeplitz(distance, tap):
    reach = jnp.abs(distance - HALF)
    total = jnp.zeros(distance.shape, F32)
    for step in range(HALF + 1):
        total = jnp.where(reach == step, tap(step), total)
    return total


def lane_of(rows):
    return lax.broadcasted_iota(jnp.int32, (rows, LANES), 1)


def kernel(
    probes, taps_in, mixing_in, nugget_in, span_in, out, quad,
    taps, mixing, nugget, span, held, land, padded, across, column_filter, row_filter, edges,
    row_halo, col_halo, corner_halo, partial, shares, slots_a, slots_b,
    param_sem, load_sem, row_send, row_recv, col_send, col_recv, corner_send, corner_recv,
    share_send, share_recv,
):
    rows, cols = held.shape[1:]
    blocks = cols // LANES
    regions, bands = lax.axis_size("region"), lax.axis_size("band")
    across_z = 8 if regions % 8 == 0 else regions
    across_x = regions // across_z
    region, band = lax.axis_index("region"), lax.axis_index("band")
    east, west = lax.rem(region + 1, regions), lax.rem(region + regions - 1, regions)
    south, north = lax.rem(band + 1, bands), lax.rem(band + bands - 1, bands)
    base_z = lax.div(region, across_z) * across_z
    at_z = lax.rem(region, across_z)

    cores = 2
    strips = bands // cores
    at_y, core = lax.div(band, cores), lax.rem(band, cores)

    def hops(step, size):
        return min(step, size - step)

    def far_first(steps, length):
        return sorted(steps, key=length, reverse=True)

    near = [
        (base_z + lax.rem(at_z + z, across_z), at_y * cores + lax.rem(core + c, cores))
        for z, c in far_first(
            [divmod(d, cores) for d in range(1, across_z * cores)],
            lambda step: hops(step[0], across_z) * cores + step[1],
        )
    ]
    far = [
        (lax.rem(region + x * across_z, regions), lax.rem(band + y * cores, bands))
        for x, y in far_first(
            [divmod(d, strips) for d in range(1, across_x * strips)],
            lambda step: hops(step[0], across_x) + hops(step[1], strips),
        )
    ]
    corners = [(east, south), (east, north), (west, south), (west, north)]
    greeted = near + far + [(region, south), (region, north), (east, band), (west, band)] + corners

    params = [
        pltpu.make_async_copy(source, target, param_sem.at[number])
        for number, (source, target) in enumerate(
            ((span_in, span), (taps_in, taps), (mixing_in, mixing), (nugget_in, nugget))
        )
    ]
    params[0].start()
    high, low = pl.ds(0, HALF), pl.ds(rows - HALF, HALF)
    middle_rows = pl.ds(HALF, rows - 2 * HALF)
    left, right = pl.ds(0, LANES), pl.ds(cols - LANES, LANES)
    whole, inside = pl.ds(0, cols), pl.ds(LANES, cols - 2 * LANES)
    every = pl.ds(0, PLANES)
    regions_of_load = [
        (every, high, whole), (every, low, whole),
        (every, middle_rows, left), (every, middle_rows, right),
    ] + [(pl.ds(VARS * p, VARS), middle_rows, inside) for p in range(PROBES)]
    loads = [
        pltpu.make_async_copy(probes.at[part], held.at[part], load_sem.at[number])
        for number, part in enumerate(regions_of_load)
    ]
    for load in loads:
        load.start()
    for param in params[1:]:
        param.start()
    barrier = pltpu.get_barrier_semaphore()
    for peer in greeted:
        pl.semaphore_signal(barrier, inc=1, device_id=peer, device_id_type=MESH)

    params[0].wait()
    def by_row(entry):
        line = span[entry].astype(F32)
        return jnp.transpose(jnp.broadcast_to(line, (LANES, rows)))

    lower, upper = by_row(0), by_row(1)
    for block in range(blocks):
        column = (lane_of(rows) + block * LANES).astype(F32)
        inside = (column >= lower) & (column < upper)
        land[:, block * LANES : (block + 1) * LANES] = jnp.where(inside, 1.0, 0.0).astype(BF16)

    lanes = lane_of(rows)
    zero = jnp.zeros((rows, LANES), BF16)
    own = slice(HALF, HALF + rows)

    def columns(j, count=1):
        return slice(j * LANES, (j + count) * LANES)

    def shifted(block, first, store):
        previous = first
        for j in range(blocks):
            current = pltpu.roll(block(j), HALF, 1)
            store(j, jnp.where(lane_of(current.shape[0]) < HALF, previous, current))
            previous = current
        return previous

    def row_copies(p):
        some = pl.ds(VARS * p, VARS)
        return [
            pltpu.make_async_remote_copy(
                held.at[some, pl.ds(rows - HALF, HALF)], row_halo.at[0, some],
                row_send.at[0, p], row_recv.at[0, p], device_id=(region, south),
                device_id_type=MESH,
            ),
            pltpu.make_async_remote_copy(
                held.at[some, pl.ds(0, HALF)], row_halo.at[1, some],
                row_send.at[1, p], row_recv.at[1, p], device_id=(region, north),
                device_id_type=MESH,
            ),
        ]

    def edge_copies(g):
        copies = []
        for side, target in ((0, west), (1, east)):
            copies.append(
                pltpu.make_async_remote_copy(
                    edges.at[side, g], col_halo.at[1 - side, g],
                    col_send.at[side, g], col_recv.at[1 - side, g],
                    device_id=(target, band), device_id_type=MESH,
                )
            )
        for side, target in ((0, west), (1, east)):
            for end, line in ((0, north), (1, south)):
                copies.append(
                    pltpu.make_async_remote_copy(
                        edges.at[side, g, pl.ds(end * (rows - HALF), HALF)],
                        corner_halo.at[1 - side, 1 - end, g],
                        corner_send.at[side, end, g], corner_recv.at[1 - side, 1 - end, g],
                        device_id=(target, line), device_id_type=MESH,
                    )
                )
        return copies

    def mask_borders(q, a, packed):
        for place in (slice(0, HALF), slice(rows - HALF, rows)):
            held[q, place] = held[q, place] * land[place]
        both = jnp.where(lanes < HALF, held[q, :, columns(0)], held[q, :, columns(blocks - 1)])
        both = both * jnp.where(lanes < HALF, land[:, columns(0)], land[:, columns(blocks - 1)])
        both = pltpu.roll(both, a * HALF, 1) if a else both
        slot = lax.div(lanes, HALF)
        return [
            jnp.where(slot == a, both, packed[0]),
            jnp.where(slot == (a - 1) % GROUP, both, packed[1]),
        ]

    def mask_and_shift(q):
        inner = slice(HALF, rows - HALF)

        def block(j):
            value = held[q, :, columns(j)] * land[:, columns(j)]
            held[q, inner, columns(j)] = value[inner]
            return value

        def store(j, value):
            padded[q, own, columns(j)] = value

        last = shifted(block, zero, store)
        store(blocks, jnp.where(lanes < HALF, last, zero))

    def filter_plane(q, chosen):
        for j in chosen:
            both = jnp.dot(
                padded[q, own, columns(j, 2)], column_filter[...], preferred_element_type=F32
            ).astype(BF16)
            for k in range(KERNELS):
                across[k, q, own, columns(j)] = both[:, columns(k)]

    row_moves, edge_moves = [], []
    for load in loads[:4]:
        load.wait()
    packed = [zero, zero]
    for p in range(PROBES):
        for q in range(VARS * p, VARS * (p + 1)):
            packed = mask_borders(q, q % GROUP, packed)
        if p == 0:
            pl.semaphore_wait(barrier, len(greeted))
        row_moves.append(row_copies(p))
        for move in row_moves[-1]:
            move.start()
        if (p + 1) * VARS % GROUP == 0:
            g = p * VARS // GROUP
            edges[0, g], edges[1, g] = packed
            packed = [zero, zero]
            edge_moves.append(edge_copies(g))
            for move in edge_moves[-1]:
                move.start()
    for param in params[1:]:
        param.wait()
    def rounded(k, axis):
        return lambda step: jnp.full((1, 1), taps[k, axis, step], F32).astype(BF16).astype(F32)

    shape = (2 * LANES, LANES)
    offset = lax.broadcasted_iota(jnp.int32, shape, 0) - lax.broadcasted_iota(jnp.int32, shape, 1)
    for k in range(KERNELS):
        column_filter[:, k * LANES : (k + 1) * LANES] = toeplitz(offset, rounded(k, 0)).astype(BF16)
    shape = (TILE, LANES)
    lane = lax.broadcasted_iota(jnp.int32, shape, 1)
    offset = lax.rem(lane, WINDOW) - lax.broadcasted_iota(jnp.int32, shape, 0)
    for k in range(KERNELS):
        pattern = toeplitz(offset, rounded(k, 1))
        for v in range(VARS):
            for w in range(0, VARS, 2):
                gains = jnp.where(lane < WINDOW, mixing[k, v, w], mixing[k, v, w + 1])
                row_filter[k, v * TILE : (v + 1) * TILE, w * WINDOW : (w + 2) * WINDOW] = (
                    gains * pattern
                ).astype(BF16)

    for q in range(PLANES):
        if q % VARS == 0:
            loads[4 + q // VARS].wait()
        mask_and_shift(q)
        filter_plane(q, range(1, blocks - 1))

    width = 2 * LANES
    partial[...] = jnp.zeros_like(partial)

    def folded(value):
        value = jnp.sum(value.reshape(-1, 8, width), axis=0)
        return value[:, :LANES] + value[:, LANES:]

    def finish_tiles(p, tiles, chunks):
        first = VARS * p
        for tile in tiles:
            own = pl.ds(tile * TILE, TILE)
            for chunk in chunks:
                part = pl.ds(chunk * width, width)
                terms = []
                for k in range(KERNELS):
                    stack = jnp.concatenate(
                        [
                            across[k, first + w, pl.ds(tile * TILE, WINDOW), part]
                            for w in range(VARS)
                        ],
                        axis=0,
                    )
                    terms.append(jnp.dot(row_filter[k], stack, preferred_element_type=F32))
                keep = land[own, part] != 0
                sums = [jnp.zeros((8, LANES), F32) for _ in range(KERNELS + 1)]
                for v in range(VARS):
                    local = held[first + v, own, part].astype(F32)
                    noise = nugget[v] * local
                    mixed = [term[v * TILE : (v + 1) * TILE] for term in terms]
                    total = (mixed[0] + mixed[1] + noise).astype(BF16)
                    out[first + v, own, part] = jnp.where(keep, total, jnp.zeros_like(total))
                    for k, term in enumerate(mixed + [noise]):
                        sums[k] = sums[k] + folded(term * local)
                for k in range(KERNELS + 1):
                    partial[k, p] = partial[k, p] + sums[k]

    pair = GROUP // VARS
    inner, outer = range(1, rows // TILE - 1), (0, rows // TILE - 1)

    def middle_tiles(g, carry):
        for p in range(pair):
            finish_tiles(pair * g + p, inner, middle)
        return carry

    chunks = cols // width
    middle, ends = range(1, chunks - 1), (0, chunks - 1)
    lax.fori_loop(0, PLANES // GROUP, middle_tiles, 0)

    def unpack(west_halo, east_halo, a):
        slot = lax.div(lane_of(west_halo.shape[0]), HALF)
        both = jnp.where(slot == a, east_halo, west_halo)
        turn = (1 - a) % GROUP * HALF
        return pltpu.roll(both, turn, 1) if turn else both

    for moves in edge_moves:
        for move in moves[:2]:
            move.wait_recv()

    def outer_columns(g, carry):
        for a in range(GROUP):
            q = GROUP * g + a
            halo = unpack(col_halo[0, g], col_halo[1, g], a)
            padded[q, own, columns(0)] = jnp.where(lanes < HALF, halo, padded[q, own, columns(0)])
            tail = jnp.where(lanes < 2 * HALF, halo, zero)
            padded[q, own, columns(blocks)] = jnp.where(
                lanes < HALF, padded[q, own, columns(blocks)], tail
            )
        for a in range(GROUP):
            filter_plane(GROUP * g + a, (0, blocks - 1))
        for p in range(pair):
            finish_tiles(pair * g + p, inner, ends)
        return carry

    lax.fori_loop(0, PLANES // GROUP, outer_columns, 0)


    beyond = [(band > 0).astype(F32).astype(BF16), (band < bands - 1).astype(F32).astype(BF16)]
    short = lane_of(HALF)
    none = jnp.zeros((HALF, LANES), BF16)
    def halo_plane(q, g, a):
        for end, place in ((0, 0), (1, HALF + rows)):
            halo = unpack(corner_halo[0, end, g], corner_halo[1, end, g], a)

            def store(j, value):
                padded[q, place : place + HALF, columns(j)] = value * beyond[end]

            last = shifted(lambda j: row_halo[end, q, :, columns(j)], halo, store)
            tail = jnp.where(short < 2 * HALF, halo, none)
            store(blocks, jnp.where(short < HALF, last, tail))

    def filter_halo(number):
        places = (0, HALF + rows)
        for j in range(blocks):
            window = jnp.concatenate(
                [
                    padded[VARS * number + v, at : at + HALF, columns(j, 2)]
                    for v in range(VARS)
                    for at in places
                ],
                axis=0,
            )
            both = jnp.dot(window, column_filter[...], preferred_element_type=F32).astype(BF16)
            for v in range(VARS):
                for end, at in enumerate(places):
                    start = (2 * v + end) * HALF
                    for k in range(KERNELS):
                        across[k, VARS * number + v, at : at + HALF, columns(j)] = both[
                            start : start + HALF, columns(k)
                        ]

    for p in range(PROBES):
        if p * VARS % GROUP == 0:
            for move in edge_moves[p * VARS // GROUP][2:]:
                move.wait_recv()
        for move in row_moves[p]:
            move.wait_recv()
        for q in range(VARS * p, VARS * (p + 1)):
            halo_plane(q, q // GROUP, q % GROUP)
        filter_halo(p)
        finish_tiles(p, outer, range(chunks))


    count = (KERNELS + 1) * PROBES
    value = jnp.sum(partial[...].reshape(count, 8, LANES), axis=1)
    value = jnp.sum(value, axis=1, keepdims=True)
    row = lax.broadcasted_iota(jnp.int32, (count, LANES), 0)
    value = jnp.sum(jnp.where(lane_of(count) == row, value, 0.0), axis=0, keepdims=True)
    share_moves = []
    for number, (peers, slots) in enumerate(((near, slots_a), (far, slots_b))):
        if not peers:
            continue
        shares[number] = value
        moves = [
            pltpu.make_async_remote_copy(
                shares.at[number], slots.at[d], share_send.at[number, d], share_recv.at[number, d],
                device_id=peer, device_id_type=MESH,
            )
            for d, peer in enumerate(peers)
        ]
        for move in moves:
            move.start()
        for move in moves:
            move.wait_recv()
        value = value + jnp.sum(slots[: len(peers)], axis=0)
        share_moves.append(moves)
    value = jnp.broadcast_to(value * (1.0 / (bands * rows * cols)), (PROBES, LANES))
    lane = lane_of(PROBES)
    row = lax.broadcasted_iota(jnp.int32, (PROBES, LANES), 0)
    for k in range(KERNELS + 1):
        chosen = jnp.where(lane == k * PROBES + row, value, 0.0)
        quad[:, k : k + 1] = jnp.sum(chosen, axis=1, keepdims=True)

    for moves in row_moves + edge_moves + share_moves:
        for move in moves:
            move.wait_send()


def per_device(probes, filter_taps, mixing, nugget, land_span):
    rows, cols = probes.shape[2:]
    any_space = pl.BlockSpec(memory_space=pl.ANY)
    vector = pl.BlockSpec(memory_space=pltpu.VMEM)
    dma = pltpu.SemaphoreType.DMA
    out, quadratic = pl.pallas_call(
        kernel,
        out_shape=(
            pltpu.VMEM((PLANES, rows, cols), BF16),
            pltpu.VMEM((PROBES, KERNELS + 1), F32),
        ),
        in_specs=[any_space] * 5,
        out_specs=(vector, vector),
        scratch_shapes=[
            pltpu.SMEM(filter_taps.shape, F32),
            pltpu.SMEM(mixing.shape, F32),
            pltpu.SMEM(nugget.shape, F32),
            pltpu.VMEM((2, 1, rows), jnp.int32),
            pltpu.VMEM((PLANES, rows, cols), BF16),
            pltpu.VMEM((rows, cols), BF16),
            pltpu.VMEM((PLANES, rows + 2 * HALF, cols + LANES), BF16),
            pltpu.VMEM((KERNELS, PLANES, rows + 2 * HALF, cols), BF16),
            pltpu.VMEM((2 * LANES, KERNELS * LANES), BF16),
            pltpu.VMEM((KERNELS, VARS * TILE, VARS * WINDOW), BF16),
            pltpu.VMEM((2, PLANES // GROUP, rows, LANES), BF16),
            pltpu.VMEM((2, PLANES, HALF, cols), BF16),
            pltpu.VMEM((2, PLANES // GROUP, rows, LANES), BF16),
            pltpu.VMEM((2, 2, PLANES // GROUP, HALF, LANES), BF16),
            pltpu.VMEM((KERNELS + 1, PROBES, 8, LANES), F32),
            pltpu.VMEM((2, 1, LANES), F32),
            pltpu.VMEM((15, 1, LANES), F32),
            pltpu.VMEM((15, 1, LANES), F32),
            dma((4,)),
            dma((4 + PROBES,)),
            dma((2, PROBES)),
            dma((2, PROBES)),
            dma((2, PLANES // GROUP)),
            dma((2, PLANES // GROUP)),
            dma((2, 2, PLANES // GROUP)),
            dma((2, 2, PLANES // GROUP)),
            dma((2, 15)),
            dma((2, 15)),
        ],
        compiler_params=pltpu.CompilerParams(
            collective_id=0, has_side_effects=True, vmem_limit_bytes=56 * 1024 * 1024
        ),
    )(
        probes.reshape(PLANES, rows, cols),
        filter_taps,
        mixing,
        nugget,
        jnp.transpose(land_span, (0, 2, 1)),
    )
    return out.reshape(PROBES, VARS, rows, cols), quadratic


def solution(mesh):
    return jax.shard_map(
        per_device,
        mesh=mesh,
        in_specs=(P(None, None, "band", "region"), P(), P(), P(), P(None, "band", "region")),
        out_specs=(P(None, None, "band", "region"), P()),
        check_vma=False,
    )
```

```python
import functools

import jax
import jax.numpy as jnp
from jax import lax
from jax.experimental import pallas as pl
from jax.experimental.pallas import tpu as pltpu
from jax.sharding import PartitionSpec as P

MESH = pl.DeviceIdType.MESH
BF16 = jnp.bfloat16
F32 = jnp.float32

PROBES, VARS, KERNELS, HALF = 4, 4, 2, 16
PLANES = PROBES * VARS
LANES = 128
TILE = 32
WINDOW = TILE + 2 * HALF
GROUP = LANES // HALF


def toeplitz(distance, tap):
    reach = jnp.abs(distance - HALF)
    total = jnp.zeros(distance.shape, F32)
    for step in range(HALF + 1):
        total = jnp.where(reach == step, tap(step), total)
    return total


def lane_of(rows):
    return lax.broadcasted_iota(jnp.int32, (rows, LANES), 1)


def kernel(
    probes, taps_in, mixing_in, nugget_in, span_in, out, quad,
    taps, mixing, nugget, span, held, land, padded, across, column_filter, row_filter, edges,
    row_halo, col_halo, corner_halo, partial, shares, slots_a, slots_b,
    param_sem, load_sem, row_send, row_recv, col_send, col_recv, corner_send, corner_recv,
    share_send, share_recv,
):
    rows, cols = held.shape[1:]
    blocks = cols // LANES
    regions, bands = lax.axis_size("region"), lax.axis_size("band")
    across_z = 8 if regions % 8 == 0 else regions
    across_x = regions // across_z
    region, band = lax.axis_index("region"), lax.axis_index("band")
    east, west = lax.rem(region + 1, regions), lax.rem(region + regions - 1, regions)
    south, north = lax.rem(band + 1, bands), lax.rem(band + bands - 1, bands)
    base_z = lax.div(region, across_z) * across_z
    at_z = lax.rem(region, across_z)

    cores = 2
    strips = bands // cores
    at_y, core = lax.div(band, cores), lax.rem(band, cores)

    def hops(step, size):
        return min(step, size - step)

    def far_first(steps, length):
        return sorted(steps, key=length, reverse=True)

    near = [
        (base_z + lax.rem(at_z + z, across_z), at_y * cores + lax.rem(core + c, cores))
        for z, c in far_first(
            [divmod(d, cores) for d in range(1, across_z * cores)],
            lambda step: hops(step[0], across_z) * cores + step[1],
        )
    ]
    far = [
        (lax.rem(region + x * across_z, regions), lax.rem(band + y * cores, bands))
        for x, y in far_first(
            [divmod(d, strips) for d in range(1, across_x * strips)],
            lambda step: hops(step[0], across_x) + hops(step[1], strips),
        )
    ]
    corners = [(east, south), (east, north), (west, south), (west, north)]
    greeted = near + far + [(region, south), (region, north), (east, band), (west, band)] + corners

    params = [
        pltpu.make_async_copy(source, target, param_sem.at[number])
        for number, (source, target) in enumerate(
            ((span_in, span), (taps_in, taps), (mixing_in, mixing), (nugget_in, nugget))
        )
    ]
    params[0].start()
    high, low = pl.ds(0, HALF), pl.ds(rows - HALF, HALF)
    middle_rows = pl.ds(HALF, rows - 2 * HALF)
    left, right = pl.ds(0, LANES), pl.ds(cols - LANES, LANES)
    whole, inside = pl.ds(0, cols), pl.ds(LANES, cols - 2 * LANES)
    every = pl.ds(0, PLANES)
    regions_of_load = [
        (every, high, whole), (every, low, whole),
        (every, middle_rows, left), (every, middle_rows, right),
    ] + [(pl.ds(VARS * p, VARS), middle_rows, inside) for p in range(PROBES)]
    loads = [
        pltpu.make_async_copy(probes.at[part], held.at[part], load_sem.at[number])
        for number, part in enumerate(regions_of_load)
    ]
    for load in loads:
        load.start()
    for param in params[1:]:
        param.start()
    barrier = pltpu.get_barrier_semaphore()
    for peer in greeted:
        pl.semaphore_signal(barrier, inc=1, device_id=peer, device_id_type=MESH)

    params[0].wait()
    def by_row(entry):
        line = span[entry].astype(F32)
        return jnp.transpose(jnp.broadcast_to(line, (LANES, rows)))

    lower, upper = by_row(0), by_row(1)
    for block in range(blocks):
        column = (lane_of(rows) + block * LANES).astype(F32)
        inside = (column >= lower) & (column < upper)
        land[:, block * LANES : (block + 1) * LANES] = jnp.where(inside, 1.0, 0.0).astype(BF16)

    lanes = lane_of(rows)
    zero = jnp.zeros((rows, LANES), BF16)
    own = slice(HALF, HALF + rows)

    def columns(j, count=1):
        return slice(j * LANES, (j + count) * LANES)

    def shifted(block, first, store):
        previous = first
        for j in range(blocks):
            current = pltpu.roll(block(j), HALF, 1)
            store(j, jnp.where(lane_of(current.shape[0]) < HALF, previous, current))
            previous = current
        return previous

    def row_copies(p):
        some = pl.ds(VARS * p, VARS)
        return [
            pltpu.make_async_remote_copy(
                held.at[some, pl.ds(rows - HALF, HALF)], row_halo.at[0, some],
                row_send.at[0, p], row_recv.at[0, p], device_id=(region, south),
                device_id_type=MESH,
            ),
            pltpu.make_async_remote_copy(
                held.at[some, pl.ds(0, HALF)], row_halo.at[1, some],
                row_send.at[1, p], row_recv.at[1, p], device_id=(region, north),
                device_id_type=MESH,
            ),
        ]

    def edge_copies(g):
        copies = []
        for side, target in ((0, west), (1, east)):
            copies.append(
                pltpu.make_async_remote_copy(
                    edges.at[side, g], col_halo.at[1 - side, g],
                    col_send.at[side, g], col_recv.at[1 - side, g],
                    device_id=(target, band), device_id_type=MESH,
                )
            )
        for side, target in ((0, west), (1, east)):
            for end, line in ((0, north), (1, south)):
                copies.append(
                    pltpu.make_async_remote_copy(
                        edges.at[side, g, pl.ds(end * (rows - HALF), HALF)],
                        corner_halo.at[1 - side, 1 - end, g],
                        corner_send.at[side, end, g], corner_recv.at[1 - side, 1 - end, g],
                        device_id=(target, line), device_id_type=MESH,
                    )
                )
        return copies

    def mask_rows(q):
        for place in (slice(0, HALF), slice(rows - HALF, rows)):
            held[q, place] = held[q, place] * land[place]

    def pack_edges(q, a, packed):
        both = jnp.where(lanes < HALF, held[q, :, columns(0)], held[q, :, columns(blocks - 1)])
        both = both * jnp.where(lanes < HALF, land[:, columns(0)], land[:, columns(blocks - 1)])
        both = pltpu.roll(both, a * HALF, 1) if a else both
        slot = lax.div(lanes, HALF)
        return [
            jnp.where(slot == a, both, packed[0]),
            jnp.where(slot == (a - 1) % GROUP, both, packed[1]),
        ]

    def mask_and_shift(q):
        inner = slice(HALF, rows - HALF)

        def block(j):
            value = held[q, :, columns(j)] * land[:, columns(j)]
            held[q, inner, columns(j)] = value[inner]
            return value

        def store(j, value):
            padded[q, own, columns(j)] = value

        last = shifted(block, zero, store)
        store(blocks, jnp.where(lanes < HALF, last, zero))

    def filter_plane(q, chosen):
        for j in chosen:
            both = jnp.dot(
                padded[q, own, columns(j, 2)], column_filter[...], preferred_element_type=F32
            ).astype(BF16)
            for k in range(KERNELS):
                across[k, q, own, columns(j)] = both[:, columns(k)]

    row_moves, edge_moves = [], []
    for load in loads[:2]:
        load.wait()
    for p in range(PROBES):
        for q in range(VARS * p, VARS * (p + 1)):
            mask_rows(q)
        if p == 0:
            pl.semaphore_wait(barrier, len(greeted))
        row_moves.append(row_copies(p))
        for move in row_moves[-1]:
            move.start()
    for load in loads[2:4]:
        load.wait()
    packed = [zero, zero]
    for p in range(PROBES):
        for q in range(VARS * p, VARS * (p + 1)):
            packed = pack_edges(q, q % GROUP, packed)
        if (p + 1) * VARS % GROUP == 0:
            g = p * VARS // GROUP
            edges[0, g], edges[1, g] = packed
            packed = [zero, zero]
            edge_moves.append(edge_copies(g))
            for move in edge_moves[-1]:
                move.start()
    for param in params[1:]:
        param.wait()
    def rounded(k, axis):
        return lambda step: jnp.full((1, 1), taps[k, axis, step], F32).astype(BF16).astype(F32)

    shape = (2 * LANES, LANES)
    offset = lax.broadcasted_iota(jnp.int32, shape, 0) - lax.broadcasted_iota(jnp.int32, shape, 1)
    for k in range(KERNELS):
        column_filter[:, k * LANES : (k + 1) * LANES] = toeplitz(offset, rounded(k, 0)).astype(BF16)
    shape = (TILE, LANES)
    lane = lax.broadcasted_iota(jnp.int32, shape, 1)
    offset = lax.rem(lane, WINDOW) - lax.broadcasted_iota(jnp.int32, shape, 0)
    for k in range(KERNELS):
        pattern = toeplitz(offset, rounded(k, 1))
        for v in range(VARS):
            for w in range(0, VARS, 2):
                gains = jnp.where(lane < WINDOW, mixing[k, v, w], mixing[k, v, w + 1])
                row_filter[k, v * TILE : (v + 1) * TILE, w * WINDOW : (w + 2) * WINDOW] = (
                    gains * pattern
                ).astype(BF16)

    for q in range(PLANES):
        if q % VARS == 0:
            loads[4 + q // VARS].wait()
        mask_and_shift(q)
        filter_plane(q, range(1, blocks - 1))

    width = 2 * LANES
    partial[...] = jnp.zeros_like(partial)

    def folded(value):
        value = jnp.sum(value.reshape(-1, 8, width), axis=0)
        return value[:, :LANES] + value[:, LANES:]

    def finish_tiles(p, tiles, chunks):
        first = VARS * p
        for tile in tiles:
            own = pl.ds(tile * TILE, TILE)
            for chunk in chunks:
                part = pl.ds(chunk * width, width)
                terms = []
                for k in range(KERNELS):
                    stack = jnp.concatenate(
                        [
                            across[k, first + w, pl.ds(tile * TILE, WINDOW), part]
                            for w in range(VARS)
                        ],
                        axis=0,
                    )
                    terms.append(jnp.dot(row_filter[k], stack, preferred_element_type=F32))
                keep = land[own, part] != 0
                sums = [jnp.zeros((8, LANES), F32) for _ in range(KERNELS + 1)]
                for v in range(VARS):
                    local = held[first + v, own, part].astype(F32)
                    noise = nugget[v] * local
                    mixed = [term[v * TILE : (v + 1) * TILE] for term in terms]
                    total = (mixed[0] + mixed[1] + noise).astype(BF16)
                    out[first + v, own, part] = jnp.where(keep, total, jnp.zeros_like(total))
                    for k, term in enumerate(mixed + [noise]):
                        sums[k] = sums[k] + folded(term * local)
                for k in range(KERNELS + 1):
                    partial[k, p] = partial[k, p] + sums[k]

    pair = GROUP // VARS
    inner, outer = range(1, rows // TILE - 1), (0, rows // TILE - 1)

    def middle_tiles(g, carry):
        for p in range(pair):
            finish_tiles(pair * g + p, inner, middle)
        return carry

    chunks = cols // width
    middle, ends = range(1, chunks - 1), (0, chunks - 1)
    lax.fori_loop(0, PLANES // GROUP, middle_tiles, 0)

    def unpack(west_halo, east_halo, a):
        slot = lax.div(lane_of(west_halo.shape[0]), HALF)
        both = jnp.where(slot == a, east_halo, west_halo)
        turn = (1 - a) % GROUP * HALF
        return pltpu.roll(both, turn, 1) if turn else both

    for moves in edge_moves:
        for move in moves[:2]:
            move.wait_recv()

    def outer_columns(g, carry):
        for a in range(GROUP):
            q = GROUP * g + a
            halo = unpack(col_halo[0, g], col_halo[1, g], a)
            padded[q, own, columns(0)] = jnp.where(lanes < HALF, halo, padded[q, own, columns(0)])
            tail = jnp.where(lanes < 2 * HALF, halo, zero)
            padded[q, own, columns(blocks)] = jnp.where(
                lanes < HALF, padded[q, own, columns(blocks)], tail
            )
        for a in range(GROUP):
            filter_plane(GROUP * g + a, (0, blocks - 1))
        for p in range(pair):
            finish_tiles(pair * g + p, inner, ends)
        return carry

    lax.fori_loop(0, PLANES // GROUP, outer_columns, 0)


    beyond = [(band > 0).astype(F32).astype(BF16), (band < bands - 1).astype(F32).astype(BF16)]
    short = lane_of(HALF)
    none = jnp.zeros((HALF, LANES), BF16)
    def halo_plane(q, g, a):
        for end, place in ((0, 0), (1, HALF + rows)):
            halo = unpack(corner_halo[0, end, g], corner_halo[1, end, g], a)

            def store(j, value):
                padded[q, place : place + HALF, columns(j)] = value * beyond[end]

            last = shifted(lambda j: row_halo[end, q, :, columns(j)], halo, store)
            tail = jnp.where(short < 2 * HALF, halo, none)
            store(blocks, jnp.where(short < HALF, last, tail))

    def filter_halo(number):
        places = (0, HALF + rows)
        for j in range(blocks):
            window = jnp.concatenate(
                [
                    padded[VARS * number + v, at : at + HALF, columns(j, 2)]
                    for v in range(VARS)
                    for at in places
                ],
                axis=0,
            )
            both = jnp.dot(window, column_filter[...], preferred_element_type=F32).astype(BF16)
            for v in range(VARS):
                for end, at in enumerate(places):
                    start = (2 * v + end) * HALF
                    for k in range(KERNELS):
                        across[k, VARS * number + v, at : at + HALF, columns(j)] = both[
                            start : start + HALF, columns(k)
                        ]

    for p in range(PROBES):
        if p * VARS % GROUP == 0:
            for move in edge_moves[p * VARS // GROUP][2:]:
                move.wait_recv()
        for move in row_moves[p]:
            move.wait_recv()
        for q in range(VARS * p, VARS * (p + 1)):
            halo_plane(q, q // GROUP, q % GROUP)
        filter_halo(p)
        finish_tiles(p, outer, range(chunks))


    count = (KERNELS + 1) * PROBES
    value = jnp.sum(partial[...].reshape(count, 8, LANES), axis=1)
    value = jnp.sum(value, axis=1, keepdims=True)
    row = lax.broadcasted_iota(jnp.int32, (count, LANES), 0)
    value = jnp.sum(jnp.where(lane_of(count) == row, value, 0.0), axis=0, keepdims=True)
    share_moves = []
    for number, (peers, slots) in enumerate(((near, slots_a), (far, slots_b))):
        if not peers:
            continue
        shares[number] = value
        moves = [
            pltpu.make_async_remote_copy(
                shares.at[number], slots.at[d], share_send.at[number, d], share_recv.at[number, d],
                device_id=peer, device_id_type=MESH,
            )
            for d, peer in enumerate(peers)
        ]
        for move in moves:
            move.start()
        for move in moves:
            move.wait_recv()
        value = value + jnp.sum(slots[: len(peers)], axis=0)
        share_moves.append(moves)
    value = jnp.broadcast_to(value * (1.0 / (bands * rows * cols)), (PROBES, LANES))
    lane = lane_of(PROBES)
    row = lax.broadcasted_iota(jnp.int32, (PROBES, LANES), 0)
    for k in range(KERNELS + 1):
        chosen = jnp.where(lane == k * PROBES + row, value, 0.0)
        quad[:, k : k + 1] = jnp.sum(chosen, axis=1, keepdims=True)

    for moves in row_moves + edge_moves + share_moves:
        for move in moves:
            move.wait_send()


def per_device(probes, filter_taps, mixing, nugget, land_span):
    rows, cols = probes.shape[2:]
    any_space = pl.BlockSpec(memory_space=pl.ANY)
    vector = pl.BlockSpec(memory_space=pltpu.VMEM)
    dma = pltpu.SemaphoreType.DMA
    out, quadratic = pl.pallas_call(
        kernel,
        out_shape=(
            pltpu.VMEM((PLANES, rows, cols), BF16),
            pltpu.VMEM((PROBES, KERNELS + 1), F32),
        ),
        in_specs=[any_space] * 5,
        out_specs=(vector, vector),
        scratch_shapes=[
            pltpu.SMEM(filter_taps.shape, F32),
            pltpu.SMEM(mixing.shape, F32),
            pltpu.SMEM(nugget.shape, F32),
            pltpu.VMEM((2, 1, rows), jnp.int32),
            pltpu.VMEM((PLANES, rows, cols), BF16),
            pltpu.VMEM((rows, cols), BF16),
            pltpu.VMEM((PLANES, rows + 2 * HALF, cols + LANES), BF16),
            pltpu.VMEM((KERNELS, PLANES, rows + 2 * HALF, cols), BF16),
            pltpu.VMEM((2 * LANES, KERNELS * LANES), BF16),
            pltpu.VMEM((KERNELS, VARS * TILE, VARS * WINDOW), BF16),
            pltpu.VMEM((2, PLANES // GROUP, rows, LANES), BF16),
            pltpu.VMEM((2, PLANES, HALF, cols), BF16),
            pltpu.VMEM((2, PLANES // GROUP, rows, LANES), BF16),
            pltpu.VMEM((2, 2, PLANES // GROUP, HALF, LANES), BF16),
            pltpu.VMEM((KERNELS + 1, PROBES, 8, LANES), F32),
            pltpu.VMEM((2, 1, LANES), F32),
            pltpu.VMEM((15, 1, LANES), F32),
            pltpu.VMEM((15, 1, LANES), F32),
            dma((4,)),
            dma((4 + PROBES,)),
            dma((2, PROBES)),
            dma((2, PROBES)),
            dma((2, PLANES // GROUP)),
            dma((2, PLANES // GROUP)),
            dma((2, 2, PLANES // GROUP)),
            dma((2, 2, PLANES // GROUP)),
            dma((2, 15)),
            dma((2, 15)),
        ],
        compiler_params=pltpu.CompilerParams(
            collective_id=0, has_side_effects=True, vmem_limit_bytes=56 * 1024 * 1024
        ),
    )(
        probes.reshape(PLANES, rows, cols),
        filter_taps,
        mixing,
        nugget,
        jnp.transpose(land_span, (0, 2, 1)),
    )
    return out.reshape(PROBES, VARS, rows, cols), quadratic


def solution(mesh):
    return jax.shard_map(
        per_device,
        mesh=mesh,
        in_specs=(P(None, None, "band", "region"), P(), P(), P(), P(None, "band", "region")),
        out_specs=(P(None, None, "band", "region"), P()),
        check_vma=False,
    )
```
